32 devices in a mesh: brow: 8 (over z, core), bcol: 4 (over y, x).
Axes of the slice: x: 2, y: 2, z: 4, core: 2. Of those that a mesh axis runs over, the one named last changes fastest.
Arguments:
- right_side: float32 [16384, 64], P(('brow', 'bcol')), may hold values from -36 to 36
- tiles: bfloat16 [64, 1, 512, 512], P(('brow', 'bcol')), may hold values from -0.03125 to 0.03125
- row_blocks: int32 [64], P(('brow', 'bcol')), may hold values from 0 to 31, as said below
- col_blocks: int32 [64, 1], P(('brow', 'bcol')), may hold values from 0 to 31, as said below
Outputs:
- solution: float32 [16384, 64], P(('brow', 'bcol'))
- residual: float32 [16384, 64], P(('brow', 'bcol'))
The draws below stay inside these ranges and needn't reach their ends.
Inputs may be any that keep to these rules, and one draw needn't show every extreme that they name: `row_blocks`: the 2 row blocks of one device lie in different groups, the group of block b being b % 4. `col_blocks`: the tile columns of the device at bcol index j are blocks c with c % 4 == j, different within one row slot.
All inputs are finite; a program needn't handle non-finite values.
Results may differ from the reference program's by a relative error of at most 0.0061.
Values may be sent and summed in bfloat16 or wider, within the bound.
A program may use at most 128 MiB of HBM per device.

```python
import math
import jax
import jax.numpy as jnp
from jax import lax

TRAITS = 64
TILE = 512
COLS_ROW = 1
ITERS = 3
GROUPS = 4
GROUP_BLOCKS = 8
BLOCKS = 32
ROW_SLOTS = 2
ROWS = 16384


def draw_row_blocks(key, part):
    keys = jax.random.split(jax.random.fold_in(key, 11), BLOCKS)
    picked = jax.vmap(lambda one: jax.random.permutation(one, GROUPS)[:ROW_SLOTS])(keys)
    places = jax.random.randint(jax.random.fold_in(key, 12), (BLOCKS, ROW_SLOTS), 0, GROUP_BLOCKS)
    return (places * GROUPS + picked).reshape(-1).astype(jnp.int32)


def draw_col_blocks(key, part):
    keys = jax.random.split(jax.random.fold_in(key, 21), BLOCKS * ROW_SLOTS)
    places = jax.vmap(lambda one: jax.random.permutation(one, GROUP_BLOCKS)[:COLS_ROW])(keys)
    owner = jnp.arange(BLOCKS * ROW_SLOTS, dtype=jnp.int32) // ROW_SLOTS
    column_group = owner % GROUPS
    return (places * GROUPS + column_group[:, None]).astype(jnp.int32)


def draw_right_side(key, part):
    rows = jnp.arange(ROWS)
    block = rows // TILE
    brow_place = (block // GROUPS).astype(jnp.float32)
    bcol_place = (block % GROUPS).astype(jnp.float32)
    ramp = 3.0 ** (brow_place / max(GROUP_BLOCKS - 1, 1)) * 3.0 ** (bcol_place / max(GROUPS - 1, 1)) / 9.0
    row_scale = jnp.exp(jax.random.uniform(jax.random.fold_in(key, 31), (ROWS,), jnp.float32, math.log(0.3), math.log(3.0)))
    col_scale = jnp.exp(jax.random.uniform(jax.random.fold_in(key, 32), (TRAITS,), jnp.float32, math.log(0.3), math.log(3.0)))
    values = jnp.clip(jax.random.normal(jax.random.fold_in(key, 33), (ROWS, TRAITS), jnp.float32), -4.0, 4.0)
    return values * row_scale[:, None] * col_scale[None, :] * ramp[:, None]


def steps_of(stream_key, shape, pieces, least, top_value):
    def one(dim, shards_of):
        steps = jax.random.uniform(jax.random.fold_in(jax.random.fold_in(stream_key, 6), dim), (shards_of,), jnp.float32, least / len(pieces), top_value / len(pieces))
        return jnp.repeat(jnp.exp(steps), shape[dim] // shards_of).reshape((-1,) + (1,) * (len(shape) - dim - 1))

    level = one(*pieces[0])
    for cut in pieces[1:]:
        level = level * one(*cut)
    return level


def gaussian(stream_key, shape, scale, reach, shards=(), held_as=jnp.bfloat16):
    level = steps_of(stream_key, shape, shards, -0.22, 0.18) if shards else 1.0
    drawn = jax.random.normal(stream_key, shape, jnp.float32) * scale * level
    return jnp.minimum(jnp.maximum(drawn, -reach), reach).astype(held_as)


def setup_inputs(seed: int = 0) -> dict:
    seeds = jax.random.split(jax.random.key(seed), 5)
    right_side = draw_right_side(jax.random.fold_in(seeds[4], 71), 0)
    tiles = gaussian(seeds[1], (BLOCKS * ROW_SLOTS, COLS_ROW, TILE, TILE), (32 * TILE * ROW_SLOTS * COLS_ROW) ** -0.5, 0.03125, ((0, 32),))
    row_blocks = draw_row_blocks(jax.random.fold_in(seeds[4], 71), 0)
    col_blocks = draw_col_blocks(jax.random.fold_in(seeds[4], 71), 0)
    return dict(right_side=right_side, tiles=tiles, row_blocks=row_blocks, col_blocks=col_blocks)


highest = lax.Precision.HIGHEST

def solve_spd(matrix, rhs):
    factor = jnp.linalg.cholesky(matrix)
    return jax.scipy.linalg.cho_solve((factor, True), rhs)

def gram_of(left, right):
    return jnp.dot(left.T, right, precision=highest)

def reference(right_side, tiles, row_blocks, col_blocks):
    width = right_side.shape[1]
    tile_rows = row_blocks.reshape(BLOCKS, ROW_SLOTS)
    tile_cols = col_blocks.reshape(BLOCKS, ROW_SLOTS, COLS_ROW)
    tile_data = tiles.reshape(BLOCKS, ROW_SLOTS, COLS_ROW, TILE, TILE)

    def apply_graph(direction):
        blocks = direction.astype(jnp.bfloat16).reshape(BLOCKS, TILE, width)

        def per_device(total, inputs):
            rows, cols, data = inputs
            weights = data.astype(jnp.float32)
            row_dir = blocks[rows].astype(jnp.float32)
            col_dir = blocks[cols].astype(jnp.float32)
            turned = jnp.einsum('scab,sak->scbk', weights, row_dir, precision=highest)
            direct = jnp.einsum('scab,scbk->sak', weights, col_dir, precision=highest)
            total = total.at[cols.reshape(-1)].add(turned.reshape(-1, TILE, width))
            total = total.at[rows].add(direct)
            return (total, None)
        start = jnp.zeros((BLOCKS, TILE, width), jnp.float32)
        total, unused = lax.scan(per_device, start, (tile_rows, tile_cols, tile_data))
        return total.reshape(ROWS, width)
    solution = jnp.zeros_like(right_side)
    residual = right_side
    direction = right_side
    rr_now = gram_of(residual, residual)
    for step in range(ITERS):
        image = 3.0 * direction + apply_graph(direction)
        alpha = solve_spd(gram_of(direction, image), rr_now)
        solution = solution + jnp.dot(direction, alpha, precision=highest)
        residual = residual - jnp.dot(image, alpha, precision=highest)
        if step + 1 < ITERS:
            fresh = gram_of(residual, residual)
            beta = solve_spd(rr_now, fresh)
            direction = residual + jnp.dot(direction, beta, precision=highest)
            rr_now = fresh
    return (solution, residual)
```

```python
import functools

import jax
import jax.numpy as jnp
from jax import lax
from jax.experimental import pallas as pl
from jax.experimental.pallas import tpu as pltpu
from jax.sharding import PartitionSpec as P

ITERS = 3
CORES = 2
MESH = pl.DeviceIdType.MESH
highest = lax.Precision.HIGHEST


def dot32(left, right, dims):
    return lax.dot_general(
        left, right, (dims, ((), ())), precision=highest, preferred_element_type=jnp.float32
    )


def dot16(left, right, dims):
    return lax.dot_general(left, right, (dims, ((), ())), preferred_element_type=jnp.float32)


def kernel(
    chips, groups, slots, per_row,
    right_ref, tiles_ref, wants_ref, cols_ref, slot_ref,
    sol_ref, res_ref,
    dir_ref, image_ref, field, outgoing, arrived, pushing, returned, asked, direct, turned,
    core_out, core_in, z_own, z_out, z_in,
    gram, gram_in, part, part_in, total, left_sys, right_sys,
    z_sem, fwd_sem, ask_sem, out_sem, back_sem, core_sem, zs_sem, gr_sem, gx_sem, gg_sem,
):
    gblocks = chips * CORES
    width = right_ref.shape[0]
    brow = lax.axis_index("brow")
    bcol = lax.axis_index("bcol")
    z = brow // CORES
    core = lax.rem(brow, CORES)
    mate = 1 - core
    rows = 2 * width // gblocks

    def at_z(zz):
        return (zz * CORES + core, bcol)

    def at_row(row):
        return (row, bcol)

    def at_col(col):
        return (brow, col)

    barrier = pltpu.get_barrier_semaphore()
    for o in range(1, gblocks):
        pl.semaphore_signal(
            barrier, inc=1, device_id=at_row(lax.rem(brow + o, gblocks)), device_id_type=MESH
        )
    for o in range(1, groups):
        pl.semaphore_signal(
            barrier, inc=1, device_id=at_col(lax.rem(bcol + o, groups)), device_id_type=MESH
        )
    pl.semaphore_wait(barrier, gblocks + groups - 2)

    def send(src, dst, sems, slot, device):
        copy = pltpu.make_async_remote_copy(
            src_ref=src, dst_ref=dst, send_sem=sems.at[0, slot], recv_sem=sems.at[1, slot],
            device_id=device, device_id_type=MESH,
        )
        copy.start()
        return copy

    asks = []
    for o in range(1, groups):
        peer = lax.rem(bcol + o, groups)
        asks.append(send(wants_ref.at[peer], asked.at[bcol], ask_sem, o, at_col(peer)))
    asked[bcol] = wants_ref[bcol]

    res_ref[...] = right_ref[...]
    dir_ref[...] = right_ref[...]
    sol_ref[...] = jnp.zeros_like(sol_ref)

    def mixed(weights, count, value):
        acc = weights(0) * value(0).astype(jnp.float32)
        for k in range(1, count):
            acc = acc + weights(k) * value(k).astype(jnp.float32)
        return acc

    for step in range(ITERS):
        own = core * chips + z
        field[own] = dir_ref[...].astype(jnp.bfloat16)
        hops = []
        for o in range(1, chips):
            hops.append(
                send(field.at[own], field.at[own], z_sem, o, at_z(lax.rem(z + o, chips)))
            )
        forwards = [send(field.at[own], field.at[own], fwd_sem, 0, (z * CORES + mate, bcol))]
        for o in range(1, chips):
            hops[o - 1].wait_recv()
            src = core * chips + lax.rem(z - o + chips, chips)
            forwards.append(
                send(field.at[src], field.at[src], fwd_sem, o, (z * CORES + mate, bcol))
            )
        if step == 0:
            for copy in asks:
                copy.wait()
        for copy in hops:
            copy.wait_send()
        for copy in forwards:
            copy.wait()

        outs = []
        for o in range(1, groups + 1):
            peer = lax.rem(bcol + o, groups)
            picked = mixed(
                lambda k: asked[peer, pl.ds(k, 1), :], gblocks, lambda k: field[k]
            ).astype(jnp.bfloat16)
            if o < groups:
                outgoing[o] = picked
                outs.append(send(outgoing.at[o], arrived.at[bcol], out_sem, o, at_col(peer)))
            else:
                arrived[bcol] = picked

        def direct_of(s, carry):
            acc = jnp.zeros((width, tiles_ref.shape[2]), jnp.float32)
            for c in range(per_row):
                at = s * per_row + c
                picked = mixed(
                    lambda k: cols_ref[at, pl.ds(k, 1), :], gblocks, lambda k: field[k]
                ).astype(jnp.bfloat16)
                acc = acc + dot16(picked, tiles_ref[s, c], ((1,), (1,)))
            direct[s] = acc
            return carry

        lax.fori_loop(0, slots, direct_of, 0)
        backs = []
        for o in range(1, groups + 1):
            peer = lax.rem(bcol + o, groups)
            picked = mixed(
                lambda s: slot_ref[s, pl.ds(peer, 1), :], slots, lambda s: direct[s]
            ).astype(jnp.bfloat16)
            if o < groups:
                pushing[o] = picked
                backs.append(send(pushing.at[o], returned.at[bcol], back_sem, o, at_col(peer)))
            else:
                returned[bcol] = picked
        for copy in outs:
            copy.wait()

        def turned_of(s, carry):
            picked = mixed(
                lambda g: slot_ref[s, pl.ds(g, 1), :], groups, lambda g: arrived[g]
            ).astype(jnp.bfloat16)
            for c in range(per_row):
                turned[s * per_row + c] = dot16(picked, tiles_ref[s, c], ((1,), (0,)))
            return carry

        lax.fori_loop(0, slots, turned_of, 0)
        for copy in backs:
            copy.wait()

        def term(place):
            return mixed(
                lambda t: cols_ref[t, pl.ds(place, 1), :], slots * per_row, lambda t: turned[t]
            ) + mixed(lambda g: asked[g, pl.ds(place, 1), :], groups, lambda g: returned[g])

        crossing = []
        for k in range(chips):
            core_out[k] = term(mate * chips + k).astype(jnp.bfloat16)
            crossing.append(
                send(core_out.at[k], core_in.at[k], core_sem, k, (z * CORES + mate, bcol))
            )
        for o in range(1, chips + 1):
            zz = lax.rem(z + o, chips)
            z_own[o - 1] = term(core * chips + zz)
        for copy in crossing:
            copy.wait()
        backs = []
        for o in range(1, chips):
            zz = lax.rem(z + o, chips)
            z_out[o] = (z_own[o - 1] + core_in[zz].astype(jnp.float32)).astype(jnp.bfloat16)
            backs.append(send(z_out.at[o], z_in.at[o], zs_sem, o, at_z(zz)))
        image = 3.0 * dir_ref[...] + z_own[chips - 1] + core_in[z].astype(jnp.float32)
        for copy in backs:
            copy.wait()
        for o in range(1, chips):
            image = image + z_in[o].astype(jnp.float32)
        image_ref[...] = image

        direction = dir_ref[...]
        residual = res_ref[...]
        over = ((1,), (1,))
        curve = 0.5 * (dot32(direction, image, over) + dot32(image, direction, over))
        gram[0:width, :] = jnp.concatenate([curve, dot32(residual, residual, over)], axis=1)
        gram[width:, :] = jnp.concatenate(
            [dot32(residual, image, over), dot32(image, image, over)], axis=1
        )

        copies = []
        for o in range(1, gblocks):
            peer = lax.rem(brow + o, gblocks)
            copies.append(
                send(
                    gram.at[pl.ds(pl.multiple_of(peer * rows, rows), rows), :],
                    gram_in.at[o], gr_sem, o, at_row(peer),
                )
            )
        acc = gram[pl.ds(pl.multiple_of(brow * rows, rows), rows), :]
        for copy in copies:
            copy.wait()
        for o in range(1, gblocks):
            acc = acc + gram_in[o]
        part[...] = acc
        part_in[bcol] = acc
        copies = []
        for o in range(1, groups):
            copies.append(
                send(part, part_in.at[bcol], gx_sem, o, at_col(lax.rem(bcol + o, groups)))
            )
        for copy in copies:
            copy.wait()
        acc = part_in[0]
        for g in range(1, groups):
            acc = acc + part_in[g]
        mine = pl.ds(pl.multiple_of(brow * rows, rows), rows)
        total[mine, :] = acc
        copies = []
        for o in range(1, gblocks):
            copies.append(
                send(
                    total.at[mine, :], total.at[mine, :], gg_sem, o,
                    at_row(lax.rem(brow + o, gblocks)),
                )
            )
        for copy in copies:
            copy.wait()

        last = step + 1 == ITERS
        lanes = lax.broadcasted_iota(jnp.int32, (width, 2 * width), 1)
        subs = lax.broadcasted_iota(jnp.int32, (width, 2 * width), 0)
        top = total[0:width, :]
        left_sys[...] = top
        if not last:
            rr_now = top[:, width:]
            bottom = total[width:, :]
            eye = (lanes[:, :width] == subs[:, :width]).astype(jnp.float32)
            right_sys[...] = jnp.concatenate([rr_now, eye], axis=1)

        def eliminate(k, carry):
            for system in (left_sys,) if last else (left_sys, right_sys):
                whole = system[...]
                row = system[pl.ds(k, 1), :]
                pivot = jnp.sum(jnp.where(lanes[0:1, :] == k, row, 0.0), axis=1, keepdims=True)
                col = jnp.sum(jnp.where(lanes == k, whole, 0.0), axis=1, keepdims=True)
                scaled = row / pivot
                system[...] = jnp.where(subs == k, scaled, whole - col * scaled)
            return carry

        lax.fori_loop(0, width, eliminate, 0)
        alpha = left_sys[...][:, width:]
        flip = ((0,), (0,))
        sol_ref[...] = sol_ref[...] + dot32(alpha, direction, flip)
        residual = residual - dot32(alpha, image_ref[...], flip)
        res_ref[...] = residual
        if not last:
            cross = dot32(bottom[:, :width], alpha, ((1,), (0,)))
            square = dot32(alpha, dot32(bottom[:, width:], alpha, ((1,), (0,))), flip)
            fresh = rr_now - cross - cross.T + square
            beta = dot32(right_sys[...][:, width:], fresh, ((1,), (0,)))
            dir_ref[...] = residual + dot32(beta, direction, flip)


def shards(right_side, tiles, row_blocks, col_blocks):
    groups = lax.axis_size("bcol")
    gblocks = lax.axis_size("brow")
    chips = gblocks // CORES
    tile, width = right_side.shape
    slots, per_row = col_blocks.shape

    def place_of(blocks):
        place = blocks // groups
        return (place % CORES) * chips + place // CORES

    def wide(hot):
        return jnp.broadcast_to(hot.astype(jnp.float32)[..., None], hot.shape + (tile,))

    group_ids = jnp.arange(groups, dtype=jnp.int32)
    place_ids = jnp.arange(gblocks, dtype=jnp.int32)
    matches = (row_blocks % groups)[:, None] == group_ids[None, :]
    at_place = place_of(row_blocks)[:, None] == place_ids[None, :]
    wants = wide(jnp.any(matches[:, :, None] & at_place[:, None, :], axis=0))
    cols = wide(place_of(col_blocks.reshape(-1))[:, None] == place_ids[None, :])
    slot_hot = wide(matches)

    half = jnp.bfloat16
    full = jnp.float32
    rows = 2 * width // gblocks
    vec = (width, tile)
    dma = pltpu.SemaphoreType.DMA
    scratch = [
        pltpu.VMEM(vec, full), pltpu.VMEM(vec, full),
        pltpu.VMEM((gblocks,) + vec, half),
        pltpu.VMEM((groups,) + vec, half), pltpu.VMEM((groups,) + vec, half),
        pltpu.VMEM((groups,) + vec, half), pltpu.VMEM((groups,) + vec, half),
        pltpu.VMEM((groups, gblocks, tile), full),
        pltpu.VMEM((slots,) + vec, full), pltpu.VMEM((slots * per_row,) + vec, full),
        pltpu.VMEM((chips,) + vec, half), pltpu.VMEM((chips,) + vec, half),
        pltpu.VMEM((chips,) + vec, full),
        pltpu.VMEM((chips,) + vec, half), pltpu.VMEM((chips,) + vec, half),
        pltpu.VMEM((2 * width, 2 * width), full),
        pltpu.VMEM((gblocks, rows, 2 * width), full),
        pltpu.VMEM((rows, 2 * width), full),
        pltpu.VMEM((groups, rows, 2 * width), full),
        pltpu.VMEM((2 * width, 2 * width), full),
        pltpu.VMEM((width, 2 * width), full), pltpu.VMEM((width, 2 * width), full),
        dma((2, chips)), dma((2, chips)), dma((2, groups)), dma((2, groups)),
        dma((2, groups)), dma((2, chips)), dma((2, chips)),
        dma((2, gblocks)), dma((2, groups)), dma((2, gblocks)),
    ]
    whole = pl.BlockSpec(memory_space=pltpu.VMEM)
    solved, left = pl.pallas_call(
        functools.partial(kernel, chips, groups, slots, per_row),
        out_shape=(jax.ShapeDtypeStruct(vec, full), jax.ShapeDtypeStruct(vec, full)),
        in_specs=[whole] * 5,
        out_specs=(whole, whole),
        scratch_shapes=scratch,
        compiler_params=pltpu.CompilerParams(
            collective_id=0, has_side_effects=True, vmem_limit_bytes=48 * 1024 * 1024
        ),
    )(right_side.T, tiles, wants, cols, slot_hot)
    return (solved.T, left.T)


def solution(mesh):
    placed = (
        P(("brow", "bcol"), None),
        P(("brow", "bcol"), None, None, None),
        P(("brow", "bcol")),
        P(("brow", "bcol"), None),
    )
    return jax.shard_map(
        shards,
        mesh=mesh,
        in_specs=placed,
        out_specs=(P(("brow", "bcol"), None), P(("brow", "bcol"), None)),
        check_vma=False,
    )
```

```python
import functools

import jax
import jax.numpy as jnp
from jax import lax
from jax.experimental import pallas as pl
from jax.experimental.pallas import tpu as pltpu
from jax.sharding import PartitionSpec as P

ITERS = 3
CORES = 2
MESH = pl.DeviceIdType.MESH
highest = lax.Precision.HIGHEST


def dot32(left, right, dims):
    return lax.dot_general(
        left, right, (dims, ((), ())), precision=highest, preferred_element_type=jnp.float32
    )


def dot16(left, right, dims):
    return lax.dot_general(left, right, (dims, ((), ())), preferred_element_type=jnp.float32)


def kernel(
    chips, groups, slots, per_row,
    right_ref, tiles_ref, wants_ref, cols_ref, slot_ref,
    sol_ref, res_ref,
    dir_ref, image_ref, field, outgoing, arrived, pushing, returned, asked, direct, turned,
    core_out, core_in, z_own, z_out, z_in,
    gram, gram_in, part, part_in, total, left_sys, right_sys,
    z_sem, fwd_sem, ask_sem, out_sem, back_sem, core_sem, zs_sem, gr_sem, gx_sem, gg_sem,
):
    gblocks = chips * CORES
    width = right_ref.shape[0]
    brow = lax.axis_index("brow")
    bcol = lax.axis_index("bcol")
    z = brow // CORES
    core = lax.rem(brow, CORES)
    mate = 1 - core
    rows = 2 * width // gblocks

    def at_z(zz):
        return (zz * CORES + core, bcol)

    def at_row(row):
        return (row, bcol)

    def at_col(col):
        return (brow, col)

    barrier = pltpu.get_barrier_semaphore()
    for o in range(1, gblocks):
        pl.semaphore_signal(
            barrier, inc=1, device_id=at_row(lax.rem(brow + o, gblocks)), device_id_type=MESH
        )
    for o in range(1, groups):
        pl.semaphore_signal(
            barrier, inc=1, device_id=at_col(lax.rem(bcol + o, groups)), device_id_type=MESH
        )
    pl.semaphore_wait(barrier, gblocks + groups - 2)

    def send(src, dst, sems, slot, device):
        copy = pltpu.make_async_remote_copy(
            src_ref=src, dst_ref=dst, send_sem=sems.at[0, slot], recv_sem=sems.at[1, slot],
            device_id=device, device_id_type=MESH,
        )
        copy.start()
        return copy

    asks = []
    for o in range(1, groups):
        peer = lax.rem(bcol + o, groups)
        asks.append(send(wants_ref.at[peer], asked.at[bcol], ask_sem, o, at_col(peer)))
    asked[bcol] = wants_ref[bcol]

    res_ref[...] = right_ref[...]
    dir_ref[...] = right_ref[...]
    sol_ref[...] = jnp.zeros_like(sol_ref)

    def mixed(weights, count, value):
        acc = weights(0) * value(0).astype(jnp.float32)
        for k in range(1, count):
            acc = acc + weights(k) * value(k).astype(jnp.float32)
        return acc

    for step in range(ITERS):
        own = core * chips + z
        field[own] = dir_ref[...].astype(jnp.bfloat16)
        hops = []
        for o in range(1, chips):
            hops.append(
                send(field.at[own], field.at[own], z_sem, o, at_z(lax.rem(z + o, chips)))
            )
        forwards = [send(field.at[own], field.at[own], fwd_sem, 0, (z * CORES + mate, bcol))]
        for o in range(1, chips):
            hops[o - 1].wait_recv()
            src = core * chips + lax.rem(z - o + chips, chips)
            forwards.append(
                send(field.at[src], field.at[src], fwd_sem, o, (z * CORES + mate, bcol))
            )
        if step == 0:
            for copy in asks:
                copy.wait()
        for copy in hops:
            copy.wait_send()
        for copy in forwards:
            copy.wait()

        outs = []
        for o in range(1, groups + 1):
            peer = lax.rem(bcol + o, groups)
            picked = mixed(
                lambda k: asked[peer, pl.ds(k, 1), :], gblocks, lambda k: field[k]
            ).astype(jnp.bfloat16)
            if o < groups:
                outgoing[o] = picked
                outs.append(send(outgoing.at[o], arrived.at[bcol], out_sem, o, at_col(peer)))
            else:
                arrived[bcol] = picked

        def direct_of(s, carry):
            acc = jnp.zeros((width, tiles_ref.shape[2]), jnp.float32)
            for c in range(per_row):
                at = s * per_row + c
                picked = mixed(
                    lambda k: cols_ref[at, pl.ds(k, 1), :], gblocks, lambda k: field[k]
                ).astype(jnp.bfloat16)
                acc = acc + dot16(picked, tiles_ref[s, c], ((1,), (1,)))
            direct[s] = acc
            return carry

        lax.fori_loop(0, slots, direct_of, 0)
        backs = []
        for o in range(1, groups + 1):
            peer = lax.rem(bcol + o, groups)
            picked = mixed(
                lambda s: slot_ref[s, pl.ds(peer, 1), :], slots, lambda s: direct[s]
            ).astype(jnp.bfloat16)
            if o < groups:
                pushing[o] = picked
                backs.append(send(pushing.at[o], returned.at[bcol], back_sem, o, at_col(peer)))
            else:
                returned[bcol] = picked
        for copy in outs:
            copy.wait()

        def turned_of(s, carry):
            picked = mixed(
                lambda g: slot_ref[s, pl.ds(g, 1), :], groups, lambda g: arrived[g]
            ).astype(jnp.bfloat16)
            for c in range(per_row):
                turned[s * per_row + c] = dot16(picked, tiles_ref[s, c], ((1,), (0,)))
            return carry

        lax.fori_loop(0, slots, turned_of, 0)
        for copy in backs:
            copy.wait()

        def term(place):
            return mixed(
                lambda t: cols_ref[t, pl.ds(place, 1), :], slots * per_row, lambda t: turned[t]
            ) + mixed(lambda g: asked[g, pl.ds(place, 1), :], groups, lambda g: returned[g])

        crossing = []
        for k in range(chips):
            core_out[k] = term(mate * chips + k)
            crossing.append(
                send(core_out.at[k], core_in.at[k], core_sem, k, (z * CORES + mate, bcol))
            )
        for o in range(1, chips + 1):
            zz = lax.rem(z + o, chips)
            z_own[o - 1] = term(core * chips + zz)
        for copy in crossing:
            copy.wait()
        backs = []
        for o in range(1, chips):
            zz = lax.rem(z + o, chips)
            z_out[o] = (z_own[o - 1] + core_in[zz]).astype(jnp.bfloat16)
            backs.append(send(z_out.at[o], z_in.at[o], zs_sem, o, at_z(zz)))
        image = 3.0 * dir_ref[...] + z_own[chips - 1] + core_in[z]
        for copy in backs:
            copy.wait()
        for o in range(1, chips):
            image = image + z_in[o].astype(jnp.float32)
        image_ref[...] = image

        direction = dir_ref[...]
        residual = res_ref[...]
        over = ((1,), (1,))
        curve = 0.5 * (dot32(direction, image, over) + dot32(image, direction, over))
        gram[0:width, :] = jnp.concatenate([curve, dot32(residual, residual, over)], axis=1)
        gram[width:, :] = jnp.concatenate(
            [dot32(residual, image, over), dot32(image, image, over)], axis=1
        )

        copies = []
        for o in range(1, gblocks):
            peer = lax.rem(brow + o, gblocks)
            copies.append(
                send(
                    gram.at[pl.ds(pl.multiple_of(peer * rows, rows), rows), :],
                    gram_in.at[o], gr_sem, o, at_row(peer),
                )
            )
        acc = gram[pl.ds(pl.multiple_of(brow * rows, rows), rows), :]
        for copy in copies:
            copy.wait()
        for o in range(1, gblocks):
            acc = acc + gram_in[o]
        part[...] = acc
        part_in[bcol] = acc
        copies = []
        for o in range(1, groups):
            copies.append(
                send(part, part_in.at[bcol], gx_sem, o, at_col(lax.rem(bcol + o, groups)))
            )
        for copy in copies:
            copy.wait()
        acc = part_in[0]
        for g in range(1, groups):
            acc = acc + part_in[g]
        mine = pl.ds(pl.multiple_of(brow * rows, rows), rows)
        total[mine, :] = acc
        copies = []
        for o in range(1, gblocks):
            copies.append(
                send(
                    total.at[mine, :], total.at[mine, :], gg_sem, o,
                    at_row(lax.rem(brow + o, gblocks)),
                )
            )
        for copy in copies:
            copy.wait()

        last = step + 1 == ITERS
        lanes = lax.broadcasted_iota(jnp.int32, (width, 2 * width), 1)
        subs = lax.broadcasted_iota(jnp.int32, (width, 2 * width), 0)
        top = total[0:width, :]
        left_sys[...] = top
        if not last:
            rr_now = top[:, width:]
            bottom = total[width:, :]
            eye = (lanes[:, :width] == subs[:, :width]).astype(jnp.float32)
            right_sys[...] = jnp.concatenate([rr_now, eye], axis=1)

        sub8 = subs[0:8, :]
        lane8 = lanes[0:8, :]

        def eliminate(band_index, carry):
            base = pl.multiple_of(band_index * 8, 8)
            for system in (left_sys,) if last else (left_sys, right_sys):
                whole = system[...]
                band = system[pl.ds(base, 8), :]
                cols, inner = [], []
                for m in range(8):
                    cols.append(
                        jnp.sum(jnp.where(lanes == base + m, whole, 0.0), axis=1, keepdims=True)
                    )
                    col = jnp.sum(jnp.where(lane8 == base + m, band, 0.0), axis=1, keepdims=True)
                    inner.append(jnp.broadcast_to(col, band.shape))
                for m in range(8):
                    inverse = 1.0 / inner[m][m : m + 1, :]
                    for later in range(m + 1, 8):
                        scaled = inner[later][m : m + 1, :] * inverse
                        inner[later] = jnp.where(
                            sub8 == m, scaled, inner[later] - inner[m] * scaled
                        )
                    scaled = band[m : m + 1, :] * inverse
                    band = jnp.where(sub8 == m, scaled, band - inner[m] * scaled)
                for m in range(8):
                    whole = whole - cols[m] * band[m : m + 1, :]
                system[...] = whole
                system[pl.ds(base, 8), :] = band
            return carry

        lax.fori_loop(0, width // 8, eliminate, 0)
        alpha = left_sys[...][:, width:]
        flip = ((0,), (0,))
        sol_ref[...] = sol_ref[...] + dot32(alpha, direction, flip)
        residual = residual - dot32(alpha, image_ref[...], flip)
        res_ref[...] = residual
        if not last:
            cross = dot32(bottom[:, :width], alpha, ((1,), (0,)))
            square = dot32(alpha, dot32(bottom[:, width:], alpha, ((1,), (0,))), flip)
            fresh = rr_now - cross - cross.T + square
            beta = dot32(right_sys[...][:, width:], fresh, ((1,), (0,)))
            dir_ref[...] = residual + dot32(beta, direction, flip)


def shards(right_side, tiles, row_blocks, col_blocks):
    groups = lax.axis_size("bcol")
    gblocks = lax.axis_size("brow")
    chips = gblocks // CORES
    tile, width = right_side.shape
    slots, per_row = col_blocks.shape

    def place_of(blocks):
        place = blocks // groups
        return (place % CORES) * chips + place // CORES

    def wide(hot):
        return jnp.broadcast_to(hot.astype(jnp.float32)[..., None], hot.shape + (tile,))

    group_ids = jnp.arange(groups, dtype=jnp.int32)
    place_ids = jnp.arange(gblocks, dtype=jnp.int32)
    matches = (row_blocks % groups)[:, None] == group_ids[None, :]
    at_place = place_of(row_blocks)[:, None] == place_ids[None, :]
    wants = wide(jnp.any(matches[:, :, None] & at_place[:, None, :], axis=0))
    cols = wide(place_of(col_blocks.reshape(-1))[:, None] == place_ids[None, :])
    slot_hot = wide(matches)

    half = jnp.bfloat16
    full = jnp.float32
    rows = 2 * width // gblocks
    vec = (width, tile)
    dma = pltpu.SemaphoreType.DMA
    scratch = [
        pltpu.VMEM(vec, full), pltpu.VMEM(vec, full),
        pltpu.VMEM((gblocks,) + vec, half),
        pltpu.VMEM((groups,) + vec, half), pltpu.VMEM((groups,) + vec, half),
        pltpu.VMEM((groups,) + vec, half), pltpu.VMEM((groups,) + vec, half),
        pltpu.VMEM((groups, gblocks, tile), full),
        pltpu.VMEM((slots,) + vec, full), pltpu.VMEM((slots * per_row,) + vec, full),
        pltpu.VMEM((chips,) + vec, full), pltpu.VMEM((chips,) + vec, full),
        pltpu.VMEM((chips,) + vec, full),
        pltpu.VMEM((chips,) + vec, half), pltpu.VMEM((chips,) + vec, half),
        pltpu.VMEM((2 * width, 2 * width), full),
        pltpu.VMEM((gblocks, rows, 2 * width), full),
        pltpu.VMEM((rows, 2 * width), full),
        pltpu.VMEM((groups, rows, 2 * width), full),
        pltpu.VMEM((2 * width, 2 * width), full),
        pltpu.VMEM((width, 2 * width), full), pltpu.VMEM((width, 2 * width), full),
        dma((2, chips)), dma((2, chips)), dma((2, groups)), dma((2, groups)),
        dma((2, groups)), dma((2, chips)), dma((2, chips)),
        dma((2, gblocks)), dma((2, groups)), dma((2, gblocks)),
    ]
    whole = pl.BlockSpec(memory_space=pltpu.VMEM)
    solved, left = pl.pallas_call(
        functools.partial(kernel, chips, groups, slots, per_row),
        out_shape=(jax.ShapeDtypeStruct(vec, full), jax.ShapeDtypeStruct(vec, full)),
        in_specs=[whole] * 5,
        out_specs=(whole, whole),
        scratch_shapes=scratch,
        compiler_params=pltpu.CompilerParams(
            collective_id=0, has_side_effects=True, vmem_limit_bytes=48 * 1024 * 1024
        ),
    )(right_side.T, tiles, wants, cols, slot_hot)
    return (solved.T, left.T)


def solution(mesh):
    placed = (
        P(("brow", "bcol"), None),
        P(("brow", "bcol"), None, None, None),
        P(("brow", "bcol")),
        P(("brow", "bcol"), None),
    )
    return jax.shard_map(
        shards,
        mesh=mesh,
        in_specs=placed,
        out_specs=(P(("brow", "bcol"), None), P(("brow", "bcol"), None)),
        check_vma=False,
    )
```

```python
import functools

import jax
import jax.numpy as jnp
from jax import lax
from jax.experimental import pallas as pl
from jax.experimental.pallas import tpu as pltpu
from jax.sharding import PartitionSpec as P

ITERS = 3
CORES = 2
MESH = pl.DeviceIdType.MESH
highest = lax.Precision.HIGHEST


def dot32(left, right, dims):
    return lax.dot_general(
        left, right, (dims, ((), ())), precision=highest, preferred_element_type=jnp.float32
    )


def dot16(left, right, dims):
    return lax.dot_general(left, right, (dims, ((), ())), preferred_element_type=jnp.float32)


def kernel(
    chips, groups, slots, per_row,
    right_ref, tiles_ref, wants_ref, cols_ref, slot_ref,
    sol_ref, res_ref,
    dir_ref, image_ref, field, outgoing, arrived, pushing, returned, asked, direct, turned,
    core_out, core_in, z_out, z_in,
    gram, gram_in, part, part_in, total, left_sys, right_sys,
    z_sem, fwd_sem, ask_sem, out_sem, back_sem, core_sem, zs_sem, gr_sem, gx_sem, gg_sem,
):
    gblocks = chips * CORES
    width = right_ref.shape[0]
    brow = lax.axis_index("brow")
    bcol = lax.axis_index("bcol")
    z = brow // CORES
    core = lax.rem(brow, CORES)
    mate = 1 - core
    rows = 2 * width // gblocks

    def at_z(zz):
        return (zz * CORES + core, bcol)

    def at_row(row):
        return (row, bcol)

    def at_col(col):
        return (brow, col)

    barrier = pltpu.get_barrier_semaphore()
    for o in range(1, gblocks):
        pl.semaphore_signal(
            barrier, inc=1, device_id=at_row(lax.rem(brow + o, gblocks)), device_id_type=MESH
        )
    for o in range(1, groups):
        pl.semaphore_signal(
            barrier, inc=1, device_id=at_col(lax.rem(bcol + o, groups)), device_id_type=MESH
        )
    pl.semaphore_wait(barrier, gblocks + groups - 2)

    def send(src, dst, sems, slot, device):
        copy = pltpu.make_async_remote_copy(
            src_ref=src, dst_ref=dst, send_sem=sems.at[0, slot], recv_sem=sems.at[1, slot],
            device_id=device, device_id_type=MESH,
        )
        copy.start()
        return copy

    asks = []
    for o in range(1, groups):
        peer = lax.rem(bcol + o, groups)
        asks.append(send(wants_ref.at[peer], asked.at[bcol], ask_sem, o, at_col(peer)))
    asked[bcol] = wants_ref[bcol]

    res_ref[...] = right_ref[...]
    dir_ref[...] = right_ref[...]
    sol_ref[...] = jnp.zeros_like(sol_ref)

    def mixed(weights, count, value):
        acc = weights(0) * value(0).astype(jnp.float32)
        for k in range(1, count):
            acc = acc + weights(k) * value(k).astype(jnp.float32)
        return acc

    for step in range(ITERS):
        own = core * chips + z
        field[own] = dir_ref[...].astype(jnp.bfloat16)
        hops = []
        for o in range(1, chips):
            hops.append(
                send(field.at[own], field.at[own], z_sem, o, at_z(lax.rem(z + o, chips)))
            )
        forwards = [send(field.at[own], field.at[own], fwd_sem, 0, (z * CORES + mate, bcol))]
        for o in range(1, chips):
            hops[o - 1].wait_recv()
            src = core * chips + lax.rem(z - o + chips, chips)
            forwards.append(
                send(field.at[src], field.at[src], fwd_sem, o, (z * CORES + mate, bcol))
            )
        if step == 0:
            for copy in asks:
                copy.wait()

        def half_of(peer, side):
            return mixed(
                lambda k: asked[peer, pl.ds(side * chips + k, 1), :],
                chips,
                lambda k: field[side * chips + k],
            )

        for o in range(1, groups + 1):
            peer = lax.rem(bcol + o, groups)
            outgoing[o % groups] = half_of(peer, core).astype(jnp.bfloat16)
        for copy in hops:
            copy.wait_send()
        for copy in forwards:
            copy.wait()

        outs = []
        for o in range(1, groups + 1):
            peer = lax.rem(bcol + o, groups)
            picked = outgoing[o % groups].astype(jnp.float32) + half_of(peer, mate)
            picked = picked.astype(jnp.bfloat16)
            if o < groups:
                outgoing[o] = picked
                outs.append(send(outgoing.at[o], arrived.at[bcol], out_sem, o, at_col(peer)))
            else:
                arrived[bcol] = picked

        def direct_of(s, carry):
            acc = jnp.zeros((width, tiles_ref.shape[2]), jnp.float32)
            for c in range(per_row):
                at = s * per_row + c
                picked = mixed(
                    lambda k: cols_ref[at, pl.ds(k, 1), :], gblocks, lambda k: field[k]
                ).astype(jnp.bfloat16)
                acc = acc + dot16(picked, tiles_ref[s, c], ((1,), (1,)))
            direct[s] = acc
            return carry

        lax.fori_loop(0, slots, direct_of, 0)
        backs = []
        for o in range(1, groups + 1):
            peer = lax.rem(bcol + o, groups)
            picked = mixed(
                lambda s: slot_ref[s, pl.ds(peer, 1), :], slots, lambda s: direct[s]
            ).astype(jnp.bfloat16)
            if o < groups:
                pushing[o] = picked
                backs.append(send(pushing.at[o], returned.at[bcol], back_sem, o, at_col(peer)))
            else:
                returned[bcol] = picked
        for copy in outs:
            copy.wait()

        def turned_of(s, carry):
            picked = mixed(
                lambda g: slot_ref[s, pl.ds(g, 1), :], groups, lambda g: arrived[g]
            ).astype(jnp.bfloat16)
            for c in range(per_row):
                turned[s * per_row + c] = dot16(picked, tiles_ref[s, c], ((1,), (0,)))
            return carry

        lax.fori_loop(0, slots, turned_of, 0)
        for copy in backs:
            copy.wait()

        def term(place):
            return mixed(
                lambda t: cols_ref[t, pl.ds(place, 1), :], slots * per_row, lambda t: turned[t]
            ) + mixed(lambda g: asked[g, pl.ds(place, 1), :], groups, lambda g: returned[g])

        crossing = []
        for o in range(1, chips + 1):
            core_out[o - 1] = term(mate * chips + lax.rem(z + o, chips))
            crossing.append(
                send(
                    core_out.at[o - 1], core_in.at[o - 1], core_sem, o - 1,
                    (z * CORES + mate, bcol),
                )
            )
        backs = []
        for o in range(1, chips):
            zz = lax.rem(z + o, chips)
            mine = term(core * chips + zz)
            crossing[o - 1].wait()
            z_out[o] = (mine + core_in[o - 1]).astype(jnp.bfloat16)
            backs.append(send(z_out.at[o], z_in.at[o], zs_sem, o, at_z(zz)))
        mine = term(core * chips + z)
        crossing[chips - 1].wait()
        image = 3.0 * dir_ref[...] + mine + core_in[chips - 1]
        for copy in backs:
            copy.wait()
        for o in range(1, chips):
            image = image + z_in[o].astype(jnp.float32)
        image_ref[...] = image

        direction = dir_ref[...]
        residual = res_ref[...]
        over = ((1,), (1,))
        curve = 0.5 * (dot32(direction, image, over) + dot32(image, direction, over))
        gram[0:width, :] = jnp.concatenate([curve, dot32(residual, residual, over)], axis=1)
        if step + 1 < ITERS:
            gram[width:, :] = jnp.concatenate(
                [dot32(residual, image, over), dot32(image, image, over)], axis=1
            )

        copies = []
        for o in range(1, gblocks):
            peer = lax.rem(brow + o, gblocks)
            copies.append(
                send(
                    gram.at[pl.ds(pl.multiple_of(peer * rows, rows), rows), :],
                    gram_in.at[o], gr_sem, o, at_row(peer),
                )
            )
        acc = gram[pl.ds(pl.multiple_of(brow * rows, rows), rows), :]
        for copy in copies:
            copy.wait()
        for o in range(1, gblocks):
            acc = acc + gram_in[o]
        part[...] = acc
        part_in[bcol] = acc
        copies = []
        for o in range(1, groups):
            copies.append(
                send(part, part_in.at[bcol], gx_sem, o, at_col(lax.rem(bcol + o, groups)))
            )
        for copy in copies:
            copy.wait()
        acc = part_in[0]
        for g in range(1, groups):
            acc = acc + part_in[g]
        mine = pl.ds(pl.multiple_of(brow * rows, rows), rows)
        total[mine, :] = acc
        copies = []
        for o in range(1, gblocks):
            copies.append(
                send(
                    total.at[mine, :], total.at[mine, :], gg_sem, o,
                    at_row(lax.rem(brow + o, gblocks)),
                )
            )
        for copy in copies:
            copy.wait()

        last = step + 1 == ITERS
        lanes = lax.broadcasted_iota(jnp.int32, (width, 2 * width), 1)
        subs = lax.broadcasted_iota(jnp.int32, (width, 2 * width), 0)
        top = total[0:width, :]
        left_sys[...] = top
        if not last:
            rr_now = top[:, width:]
            bottom = total[width:, :]
            eye = (lanes[:, :width] == subs[:, :width]).astype(jnp.float32)
            right_sys[...] = jnp.concatenate([rr_now, eye], axis=1)

        sub8 = subs[0:8, :]
        lane8 = lanes[0:8, :]

        def eliminate(band_index, carry):
            base = pl.multiple_of(band_index * 8, 8)
            for system in (left_sys,) if last else (left_sys, right_sys):
                whole = system[...]
                band = system[pl.ds(base, 8), :]
                cols, inner = [], []
                for m in range(8):
                    cols.append(
                        jnp.sum(jnp.where(lanes == base + m, whole, 0.0), axis=1, keepdims=True)
                    )
                    col = jnp.sum(jnp.where(lane8 == base + m, band, 0.0), axis=1, keepdims=True)
                    inner.append(jnp.broadcast_to(col, band.shape))
                for m in range(8):
                    inverse = 1.0 / inner[m][m : m + 1, :]
                    for later in range(m + 1, 8):
                        scaled = inner[later][m : m + 1, :] * inverse
                        inner[later] = jnp.where(
                            sub8 == m, scaled, inner[later] - inner[m] * scaled
                        )
                    scaled = band[m : m + 1, :] * inverse
                    band = jnp.where(sub8 == m, scaled, band - inner[m] * scaled)
                for m in range(8):
                    whole = whole - cols[m] * band[m : m + 1, :]
                system[...] = whole
                system[pl.ds(base, 8), :] = band
            return carry

        lax.fori_loop(0, width // 8, eliminate, 0)
        alpha = left_sys[...][:, width:]
        flip = ((0,), (0,))
        sol_ref[...] = sol_ref[...] + dot32(alpha, direction, flip)
        residual = residual - dot32(alpha, image_ref[...], flip)
        res_ref[...] = residual
        if not last:
            cross = dot32(bottom[:, :width], alpha, ((1,), (0,)))
            square = dot32(alpha, dot32(bottom[:, width:], alpha, ((1,), (0,))), flip)
            fresh = rr_now - cross - cross.T + square
            beta = dot32(right_sys[...][:, width:], fresh, ((1,), (0,)))
            dir_ref[...] = residual + dot32(beta, direction, flip)


def shards(right_side, tiles, row_blocks, col_blocks):
    groups = lax.axis_size("bcol")
    gblocks = lax.axis_size("brow")
    chips = gblocks // CORES
    tile, width = right_side.shape
    slots, per_row = col_blocks.shape

    def place_of(blocks):
        place = blocks // groups
        return (place % CORES) * chips + place // CORES

    def wide(hot):
        return jnp.broadcast_to(hot.astype(jnp.float32)[..., None], hot.shape + (tile,))

    group_ids = jnp.arange(groups, dtype=jnp.int32)
    place_ids = jnp.arange(gblocks, dtype=jnp.int32)
    matches = (row_blocks % groups)[:, None] == group_ids[None, :]
    at_place = place_of(row_blocks)[:, None] == place_ids[None, :]
    wants = wide(jnp.any(matches[:, :, None] & at_place[:, None, :], axis=0))
    cols = wide(place_of(col_blocks.reshape(-1))[:, None] == place_ids[None, :])
    slot_hot = wide(matches)

    half = jnp.bfloat16
    full = jnp.float32
    rows = 2 * width // gblocks
    vec = (width, tile)
    dma = pltpu.SemaphoreType.DMA
    scratch = [
        pltpu.VMEM(vec, full), pltpu.VMEM(vec, full),
        pltpu.VMEM((gblocks,) + vec, half),
        pltpu.VMEM((groups,) + vec, half), pltpu.VMEM((groups,) + vec, half),
        pltpu.VMEM((groups,) + vec, half), pltpu.VMEM((groups,) + vec, half),
        pltpu.VMEM((groups, gblocks, tile), full),
        pltpu.VMEM((slots,) + vec, full), pltpu.VMEM((slots * per_row,) + vec, full),
        pltpu.VMEM((chips,) + vec, full), pltpu.VMEM((chips,) + vec, full),
        pltpu.VMEM((chips,) + vec, half), pltpu.VMEM((chips,) + vec, half),
        pltpu.VMEM((2 * width, 2 * width), full),
        pltpu.VMEM((gblocks, rows, 2 * width), full),
        pltpu.VMEM((rows, 2 * width), full),
        pltpu.VMEM((groups, rows, 2 * width), full),
        pltpu.VMEM((2 * width, 2 * width), full),
        pltpu.VMEM((width, 2 * width), full), pltpu.VMEM((width, 2 * width), full),
        dma((2, chips)), dma((2, chips)), dma((2, groups)), dma((2, groups)),
        dma((2, groups)), dma((2, chips)), dma((2, chips)),
        dma((2, gblocks)), dma((2, groups)), dma((2, gblocks)),
    ]
    whole = pl.BlockSpec(memory_space=pltpu.VMEM)
    solved, left = pl.pallas_call(
        functools.partial(kernel, chips, groups, slots, per_row),
        out_shape=(jax.ShapeDtypeStruct(vec, full), jax.ShapeDtypeStruct(vec, full)),
        in_specs=[whole] * 5,
        out_specs=(whole, whole),
        scratch_shapes=scratch,
        compiler_params=pltpu.CompilerParams(
            collective_id=0, has_side_effects=True, vmem_limit_bytes=48 * 1024 * 1024
        ),
    )(right_side.T, tiles, wants, cols, slot_hot)
    return (solved.T, left.T)


def solution(mesh):
    placed = (
        P(("brow", "bcol"), None),
        P(("brow", "bcol"), None, None, None),
        P(("brow", "bcol")),
        P(("brow", "bcol"), None),
    )
    return jax.shard_map(
        shards,
        mesh=mesh,
        in_specs=placed,
        out_specs=(P(("brow", "bcol"), None), P(("brow", "bcol"), None)),
        check_vma=False,
    )
```
